256 devices in a mesh: row: 16 (over y, x_hi, core), col: 8 (over z), depth: 2 (over x_lo).
Axes of the slice: x: 4 (x_hi: 2, x_lo: 2; x = x_hi * 2 + x_lo), y: 4, z: 8, core: 2. Of those that a mesh axis runs over, the one named last changes fastest.
Arguments:
- covariance: float32 [7168, 7168], P('row', 'col'), may hold values from -1 to 5, as said below
- iterate: float32 [7168, 7168], P('row', 'col'), may hold values from -1 to 1.5
Outputs:
- refreshed: float32 [7168, 4096], P(('row', 'depth'), 'col')
The draws below stay inside these ranges and needn't reach their ends.
Inputs may be any that keep to these rules, and one draw needn't show every extreme that they name: `covariance`: symmetric.
All inputs are finite; a program needn't handle non-finite values.
Results may differ from the reference program's by a relative error of at most 0.00008.
Values sent between devices are 32-bit elements; how exact they have to be, the bound alone decides.
No kernel may reach another device: no remote copies, remote signals or barrier semaphores. Data moves between devices by JAX's collectives and lax.ppermute only.
A program may use at most 64 MiB of HBM per device.

```python
import math
import jax
import jax.numpy as jnp
from jax import lax

N = 7168
PERIOD = 896
SLAB = 512
WINDOW = 4096


def diagonal_values(key):
    key = jax.random.fold_in(key, 11)
    logs = jax.random.uniform(key, (N,), jnp.float32, 0.0, math.log(4.0))
    return jnp.exp(logs)


def symmetric_noise(noise, scale):
    return (noise + noise.T) * (0.7071068 * scale / math.sqrt(N))


def draw_covariance(key, part):
    damped = diagonal_values(key)
    key = jax.random.fold_in(key, 3)
    noise = jax.random.truncated_normal(key, -6.0, 6.0, (N, N), jnp.float32)
    return symmetric_noise(noise, 0.25) + jnp.diag(damped)


def draw_iterate(key, part):
    damped = diagonal_values(key)
    key = jax.random.fold_in(key, 5)
    noise = jax.random.truncated_normal(key, -6.0, 6.0, (N, N), jnp.float32)
    return noise * (0.05 / math.sqrt(N)) + jnp.diag(1.0 / damped)


def setup_inputs(seed: int = 0) -> dict:
    keys = jax.random.split(jax.random.key(seed), 3)
    covariance = draw_covariance(jax.random.fold_in(keys[2], 71), 0)
    iterate = draw_iterate(jax.random.fold_in(keys[2], 71), 0)
    return {"covariance": covariance, "iterate": iterate}


def reference(covariance, iterate):
    positions = jnp.arange(WINDOW, dtype=jnp.int32)
    window = (positions // SLAB) * PERIOD + positions % SLAB
    window_cols = jnp.take(iterate, window, axis=1)
    product = jnp.dot(covariance, window_cols, precision=lax.Precision.HIGHEST, preferred_element_type=jnp.float32)
    indices = jnp.arange(N, dtype=jnp.int32)
    select = (indices[:, None] == window[None, :]).astype(jnp.float32)
    residual = 2.0 * select - product
    return jnp.dot(iterate, residual, precision=lax.Precision.HIGHEST, preferred_element_type=jnp.float32)
```

```python
import functools
import jax
import jax.numpy as jnp
from jax import lax
from jax.experimental import pallas as pl
from jax.experimental.pallas import tpu as pltpu
from jax.sharding import PartitionSpec as P

PERIOD = 896
SLAB = 512
F32 = jnp.float32
BF16 = jnp.bfloat16
VMEM_LIMIT = 48 * 1024 * 1024


def split(value):
    hi = value.astype(BF16)
    lo = (value - hi.astype(F32)).astype(BF16)
    return hi, lo


def dot3(a_hi, a_lo, b_hi, b_lo):
    dot = functools.partial(jnp.dot, preferred_element_type=F32)
    return dot(a_hi, b_hi) + (dot(a_hi, b_lo) + dot(a_lo, b_hi))


def lower_lanes(shape):
    return lax.broadcasted_iota(jnp.int32, shape, len(shape) - 1) < 64


def swap(value):
    return pltpu.roll(value, 64, axis=value.ndim - 1)


def row_offset(scal, block):
    half, part, first, second = block // 8, block // 4 % 2, block // 2 % 2, block % 2
    core, b1, b2 = scal[0], scal[3], scal[4]
    half = core if half else 1 - core
    b1_first, b2_first = (b1, b2) if part == 0 else (b2, b1)
    first = b1_first if first else 1 - b1_first
    second = b2_first if second else 1 - b2_first
    return pl.multiple_of(half * 448 + part * 224 + first * 112 + second * 56, 8)


def transpose_kernel(scal, tile, hi, lo, turned, ordered):
    turned[...] = tile[...].T
    for block in range(16):
        ordered[block * 56 : block * 56 + 56] = turned[pl.ds(row_offset(scal, block), 56)]
    hi[...], lo[...] = split(ordered[...])


def transposed(scal, tile):
    rows, cols = tile.shape
    return pl.pallas_call(
        transpose_kernel,
        grid_spec=pltpu.PrefetchScalarGridSpec(
            num_scalar_prefetch=1,
            grid=(1,),
            in_specs=[pl.BlockSpec((rows, cols), lambda i, s: (0, 0))],
            out_specs=[pl.BlockSpec((cols, rows), lambda i, s: (0, 0))] * 2,
            scratch_shapes=[pltpu.VMEM((cols, rows), F32)] * 2,
        ),
        out_shape=[jax.ShapeDtypeStruct((cols, rows), BF16)] * 2,
        compiler_params=pltpu.CompilerParams(vmem_limit_bytes=VMEM_LIMIT),
        cost_estimate=pl.CostEstimate(flops=0, bytes_accessed=8 * rows * cols, transcendentals=0),
        name="transpose_split",
    )(scal, tile)


def first_kernel(gathered, own_hi, own_lo, par_hi, par_lo, send, keep, w_hi, w_lo):
    step = pl.program_id(0)

    @pl.when(step == 0)
    def _():
        lower = lower_lanes((448, 128))
        for pair in range(4):
            even, odd = gathered[2 * pair], gathered[2 * pair + 1]
            cols = slice(pair * 128, pair * 128 + 128)
            own = jnp.where(lower, even, swap(odd))
            par = jnp.where(lower, swap(even), odd)
            w_hi[:448, cols], w_lo[:448, cols] = split(own)
            w_hi[448:, cols], w_lo[448:, cols] = split(par)

    total = dot3(own_hi[...], own_lo[...], w_hi[:448], w_lo[:448])
    total += dot3(par_hi[...], par_lo[...], w_hi[448:], w_lo[448:])

    @pl.when(step < 2)
    def _():
        send[...] = total

    @pl.when(step >= 2)
    def _():
        keep[...] = total


def first_product(gathered, own, par):
    tile = pl.BlockSpec((224, 448), lambda m: (m, 0))
    return pl.pallas_call(
        first_kernel,
        grid=(4,),
        in_specs=[pl.BlockSpec((8, 448, 128), lambda m: (0, 0, 0))] + [tile] * 4,
        out_specs=[
            pl.BlockSpec((224, 512), lambda m: (jnp.minimum(m, 1), 0)),
            pl.BlockSpec((224, 512), lambda m: (jnp.maximum(m - 2, 0), 0)),
        ],
        scratch_shapes=[pltpu.VMEM((896, 512), BF16)] * 2,
        out_shape=[jax.ShapeDtypeStruct((448, 512), F32)] * 2,
        compiler_params=pltpu.CompilerParams(vmem_limit_bytes=VMEM_LIMIT),
        cost_estimate=pl.CostEstimate(
            flops=6 * 896 * 896 * 512, bytes_accessed=7 << 20, transcendentals=0
        ),
        name="first_product",
    )(gathered, *own, *par)


def second_kernel(scal, other, mine, own, par, out, ordered, p_hi, p_lo):
    @pl.when(pl.program_id(0) == 0)
    def _():
        for block in range(16):
            source = other if block < 8 else mine
            start = block % 8 * 56
            ordered[pl.ds(row_offset(scal, block), 56)] = source[start : start + 56]
        p_hi[...], p_lo[...] = split(ordered[...])

    own_total = dot3(*split(own[...]), p_hi[...], p_lo[...])
    par_total = dot3(*split(par[...]), p_hi[...], p_lo[...])
    lower = lower_lanes((112, 128))
    for pair in range(4):
        cols = slice(pair * 128, pair * 128 + 128)
        a, b = own_total[:, cols], par_total[:, cols]
        out[2 * pair] = jnp.where(lower, a, swap(b))
        out[2 * pair + 1] = jnp.where(lower, swap(a), b)


def second_product(scal, other, mine, own, par):
    half = pl.BlockSpec((448, 512), lambda m, s: (0, 0))
    rows = pl.BlockSpec((112, 896), lambda m, s: ((m + 2 * (1 - s[1])) % 4, 0))
    return pl.pallas_call(
        second_kernel,
        grid_spec=pltpu.PrefetchScalarGridSpec(
            num_scalar_prefetch=1,
            grid=(4,),
            in_specs=[half, half, rows, rows],
            out_specs=pl.BlockSpec((8, 112, 128), lambda m, s: (0, m, 0)),
            scratch_shapes=[pltpu.VMEM((896, 512), F32)] + [pltpu.VMEM((896, 512), BF16)] * 2,
        ),
        out_shape=jax.ShapeDtypeStruct((8, 448, 128), F32),
        compiler_params=pltpu.CompilerParams(vmem_limit_bytes=VMEM_LIMIT),
        cost_estimate=pl.CostEstimate(
            flops=6 * 896 * 896 * 512, bytes_accessed=7 << 20, transcendentals=0
        ),
        name="second_product",
    )(scal, other, mine, own, par)


def last_kernel(scal, iterate, *refs):
    out = refs[-1]
    pieces = refs[:-1]
    x = scal[2]
    rows = pl.ds(pl.multiple_of(scal[1] * 224, 8), 224)
    lower = lower_lanes((224, 128))
    for k in range(4):
        a, b = pieces[k][...], pieces[4 + k][...]
        quarter = (x, 3 - x, x ^ 1, x ^ 2)[k]
        if k in (0, 2):
            value = jnp.where(lower, a, swap(b))
        else:
            value = jnp.where(lower, swap(a), b)
        cols = pl.ds(pl.multiple_of(quarter * 128, 128), 128)
        out[:, cols] = 2.0 * iterate[rows, cols] - value


def last(scal, iterate, pieces):
    piece = pl.BlockSpec((224, 128), lambda i, s: (0, 0))
    mine = pl.BlockSpec((224, 128), lambda i, s: (1, 0))
    return pl.pallas_call(
        last_kernel,
        grid_spec=pltpu.PrefetchScalarGridSpec(
            num_scalar_prefetch=1,
            grid=(1,),
            in_specs=[pl.BlockSpec((448, 512), lambda i, s: (0, 0))] + ([mine] + [piece] * 3) * 2,
            out_specs=pl.BlockSpec((224, 512), lambda i, s: (0, 0)),
        ),
        out_shape=jax.ShapeDtypeStruct((224, 512), F32),
        compiler_params=pltpu.CompilerParams(vmem_limit_bytes=VMEM_LIMIT),
        cost_estimate=pl.CostEstimate(flops=0, bytes_accessed=2 << 20, transcendentals=0),
        name="last",
    )(scal, iterate, *pieces)


def flip(mask):
    return [(r, r ^ mask) for r in range(16)]


def x_mirror():
    pairs = []
    for r in range(16):
        for d in range(2):
            x = 3 - ((r // 2 % 2) * 2 + d)
            pairs.append((r * 2 + d, ((r & 13) | (x // 2) * 2) * 2 + x % 2))
    return pairs


to_core = functools.partial(lax.ppermute, axis_name="row", perm=flip(1))
to_y1 = functools.partial(lax.ppermute, axis_name="row", perm=flip(4))
to_y3 = functools.partial(lax.ppermute, axis_name="row", perm=flip(12))
to_x2 = functools.partial(lax.ppermute, axis_name="row", perm=flip(2))
to_x1 = functools.partial(lax.ppermute, axis_name="depth", perm=[(0, 1), (1, 0)])
to_mirror = functools.partial(lax.ppermute, axis_name=("row", "depth"), perm=x_mirror())


def summed(send, keep):
    got = to_core(send)
    total = keep + got
    first, second = total[:224], total[224:]
    r1, r2 = to_y1(first[:112]), to_y3(second[:112])
    first, second = first[112:] + r1, second[112:] + r2
    s1, s2 = to_y3(first[:56]), to_y1(second[:56])
    first, second = first[56:] + s1, second[56:] + s2
    first = jnp.concatenate([to_y3(first), first], 0)
    second = jnp.concatenate([to_y1(second), second], 0)
    mine = jnp.concatenate([to_y1(first), first, to_y3(second), second], 0)
    return to_core(mine), mine


def local(covariance, iterate):
    row = lax.axis_index("row")
    depth = lax.axis_index("depth")
    y, x = row // 4, (row // 2 % 2) * 2 + depth
    b1, b2 = (y ^ (y // 2)) & 1, y // 2
    scal = jnp.stack([row % 2, depth, x, b1, b2]).astype(jnp.int32)

    window = iterate[:, :SLAB]
    own_w = lax.dynamic_slice_in_dim(window, x * 128, 128, 1)
    par_w = to_mirror(lax.dynamic_slice_in_dim(window, (3 - x) * 128, 128, 1))
    par_cov = to_mirror(covariance)
    par_iter = to_mirror(iterate)
    own_a = transposed(scal, covariance)
    par_a = transposed(scal, par_cov)

    packs = [
        jnp.concatenate([own_w[:, c : c + 64], par_w[:, c : c + 64]], 1) for c in (0, 64)
    ]
    pieces = []
    for pack in packs:
        gathered = lax.all_gather(pack, "col", axis=0)
        other, mine = summed(*first_product(gathered, own_a, par_a))
        result = second_product(scal, other, mine, iterate, par_iter)
        result = lax.psum_scatter(result, "col", scatter_dimension=0)
        away, home = result[:224], result[224:]
        pieces += [result, to_mirror(away), to_x1(away), to_x2(home)]
    return last(scal, iterate, pieces)


def solution(mesh):
    in_specs = (P("row", "col"), P("row", "col"))
    out_specs = P(("row", "depth"), "col")
    return jax.shard_map(local, mesh=mesh, in_specs=in_specs, out_specs=out_specs, check_vma=False)
```

```python
import functools
import jax
import jax.numpy as jnp
from jax import lax
from jax.experimental import pallas as pl
from jax.experimental.pallas import tpu as pltpu
from jax.sharding import PartitionSpec as P

F32 = jnp.float32
BF16 = jnp.bfloat16
VMEM_LIMIT = 24 * 1024 * 1024
ROWS = 448
COLS = 896
PIECE = 112
BLOCK = 128
TURNS = (1, 3, 2, 0)
together = lax.optimization_barrier


def split(value):
    hi = value.astype(BF16)
    lo = (value - hi.astype(F32)).astype(BF16)
    return hi, lo


def dot3(a_hi, a_lo, b_hi, b_lo):
    dot = functools.partial(jnp.dot, preferred_element_type=F32)
    return dot(a_hi, b_hi) + (dot(a_hi, b_lo) + dot(a_lo, b_hi))


def params():
    return pltpu.CompilerParams(vmem_limit_bytes=VMEM_LIMIT)


def piece_row(scal, core, turn):
    return pl.multiple_of(core * ROWS + (scal[3] + turn) % 4 * PIECE, PIECE)


def transpose_kernel(scal, tile, hi, lo, turned):
    turned[...] = tile[...].T
    for half, core in enumerate((1 - scal[0], scal[0])):
        for k, turn in enumerate(TURNS):
            start = half * ROWS + k * PIECE
            rows = turned[pl.ds(piece_row(scal, core, turn), PIECE)]
            hi[start : start + PIECE], lo[start : start + PIECE] = split(rows)


def transposed(scal, tile):
    return pl.pallas_call(
        transpose_kernel,
        grid_spec=pltpu.PrefetchScalarGridSpec(
            num_scalar_prefetch=1,
            grid=(1,),
            in_specs=[pl.BlockSpec((ROWS, COLS), lambda i, s: (0, 0))],
            out_specs=[pl.BlockSpec((COLS, ROWS), lambda i, s: (0, 0))] * 2,
            scratch_shapes=[pltpu.VMEM((COLS, ROWS), F32)],
        ),
        out_shape=[jax.ShapeDtypeStruct((COLS, ROWS), BF16)] * 2,
        compiler_params=params(),
        cost_estimate=pl.CostEstimate(flops=0, bytes_accessed=1024, transcendentals=0),
        name="transpose_split",
    )(scal, tile)


def first_kernel(count, *refs):
    blocks, (own_hi, own_lo, par_hi, par_lo, send, keep, w_hi, w_lo) = refs[: 2 * count], refs[2 * count :]
    for k in range(count):
        cols = slice(k * BLOCK, k * BLOCK + BLOCK)
        w_hi[:ROWS, cols], w_lo[:ROWS, cols] = split(blocks[k][...])
        w_hi[ROWS:, cols], w_lo[ROWS:, cols] = split(blocks[count + k][...])
    for half, out in enumerate((send, keep)):
        rows = slice(half * ROWS, half * ROWS + ROWS)
        total = dot3(own_hi[rows], own_lo[rows], w_hi[:ROWS], w_lo[:ROWS])
        total += dot3(par_hi[rows], par_lo[rows], w_hi[ROWS:], w_lo[ROWS:])
        out[...] = total.reshape(out.shape)


def cost(width):
    return pl.CostEstimate(
        flops=width, bytes_accessed=width, transcendentals=0
    )


def first_product(own_blocks, par_blocks, own, par):
    count = len(own_blocks)
    width = count * BLOCK
    tile = pl.BlockSpec((COLS, ROWS), lambda m: (0, 0))
    whole = pl.BlockSpec((ROWS, BLOCK), lambda m: (0, 0))
    return pl.pallas_call(
        functools.partial(first_kernel, count),
        grid=(1,),
        in_specs=[whole] * (2 * count) + [tile] * 4,
        out_specs=[pl.BlockSpec((4, PIECE, width), lambda m: (0, 0, 0))] * 2,
        scratch_shapes=[pltpu.VMEM((COLS, width), BF16)] * 2,
        out_shape=[jax.ShapeDtypeStruct((4, PIECE, width), F32)] * 2,
        compiler_params=params(),
        cost_estimate=cost(width),
        name="first_product",
    )(*own_blocks, *par_blocks, *own, *par)


def second_kernel(count, scal, *refs):
    pieces, tiles, refs = refs[:8], refs[8:10], refs[10:]
    outs, (p_hi, p_lo) = (refs[:count], refs[count : 2 * count]), refs[2 * count :]
    for half, core in enumerate((scal[0], 1 - scal[0])):
        for k, turn in enumerate((0, 3, 1, 2)):
            rows = pl.ds(piece_row(scal, core, turn), PIECE)
            p_hi[rows], p_lo[rows] = split(pieces[4 * half + k][...])
    for tile, out in zip(tiles, outs):
        for half, depth in enumerate((1 - scal[1], scal[1])):
            rows = pl.ds(pl.multiple_of(depth * (ROWS // 2), 8), ROWS // 2)
            total = dot3(*split(tile[rows]), p_hi[...], p_lo[...])
            rows = slice(half * (ROWS // 2), (half + 1) * (ROWS // 2))
            for k in range(count):
                out[k][rows] = total[:, k * BLOCK : k * BLOCK + BLOCK]


def second_product(scal, pieces, own, par):
    width = pieces[0].shape[1]
    count = width // BLOCK
    piece = pl.BlockSpec((PIECE, width), lambda m, s: (0, 0))
    tile = pl.BlockSpec((ROWS, COLS), lambda m, s: (0, 0))
    out = pl.pallas_call(
        functools.partial(second_kernel, count),
        grid_spec=pltpu.PrefetchScalarGridSpec(
            num_scalar_prefetch=1,
            grid=(1,),
            in_specs=[piece] * 8 + [tile, tile],
            out_specs=[pl.BlockSpec((ROWS, BLOCK), lambda m, s: (0, 0))] * (2 * count),
            scratch_shapes=[pltpu.VMEM((COLS, width), BF16)] * 2,
        ),
        out_shape=[jax.ShapeDtypeStruct((ROWS, BLOCK), F32)] * (2 * count),
        compiler_params=params(),
        cost_estimate=cost(width),
        name="second_product",
    )(scal, *pieces, own, par)
    return out[:count], out[count:]


def last_kernel(scal, iterate, *refs):
    pieces, out = refs[:4], refs[4]
    x = scal[2]
    rows = pl.ds(pl.multiple_of(scal[1] * 224, 8), 224)
    for piece, quarter in zip(pieces, (x, x ^ 1, 3 - x, x ^ 2)):
        cols = pl.ds(pl.multiple_of(quarter * BLOCK, BLOCK), BLOCK)
        out[:, cols] = 2.0 * iterate[rows, cols] - piece[...]


def last(scal, iterate, pieces):
    piece = pl.BlockSpec((224, BLOCK), lambda i, s: (0, 0))
    return pl.pallas_call(
        last_kernel,
        grid_spec=pltpu.PrefetchScalarGridSpec(
            num_scalar_prefetch=1,
            grid=(1,),
            in_specs=[pl.BlockSpec((ROWS, 512), lambda i, s: (0, 0))] + [piece] * 4,
            out_specs=pl.BlockSpec((224, 512), lambda i, s: (0, 0)),
        ),
        out_shape=jax.ShapeDtypeStruct((224, 512), F32),
        compiler_params=params(),
        cost_estimate=pl.CostEstimate(flops=0, bytes_accessed=1024, transcendentals=0),
        name="last",
    )(scal, iterate, *pieces)


def flip(mask):
    return [(r, r ^ mask) for r in range(16)]


def x_mirror():
    pairs = []
    for r in range(16):
        for d in range(2):
            x = 3 - ((r // 2 % 2) * 2 + d)
            pairs.append((r * 2 + d, ((r & 13) | (x // 2) * 2) * 2 + x % 2))
    return pairs


to_core = functools.partial(lax.ppermute, axis_name="row", perm=flip(1))
to_x2 = functools.partial(lax.ppermute, axis_name="row", perm=flip(2))
to_x1 = functools.partial(lax.ppermute, axis_name="depth", perm=[(0, 1), (1, 0)])
to_mirror = functools.partial(lax.ppermute, axis_name=("row", "depth"), perm=x_mirror())


def to_y(value, turn):
    return lax.ppermute(value, "row", [(r, (r + 4 * turn) % 16) for r in range(16)])


def to_z(value, turn):
    return lax.ppermute(value, "col", [(z, (z + turn) % 8) for z in range(8)])


def reduced(send, keep):
    got = to_core(send)
    pieces = together(tuple(keep[k] + got[k] for k in range(4)))
    got = together(tuple(to_y(pieces[k], TURNS[k]) for k in range(3)))
    return pieces[3] + got[0] + got[1] + got[2]


def spread(mine):
    return [mine] + [to_y(mine, turn) for turn in (1, 3, 2)]


def gathered(block, right, left):
    blocks = {0: block}
    for turn, steps in ((1, right), (-1, left)):
        value = block
        for step in range(1, steps + 1):
            value = to_z(value, turn)
            blocks[-turn * step] = value
    return blocks


def scattered(terms, right, left):
    total = terms[0]
    for turn, steps in ((1, right), (-1, left)):
        value = to_z(terms[turn * steps], turn)
        for step in range(steps - 1, 0, -1):
            value = to_z(value + terms[turn * step], turn)
        total = total + value
    return total


def local(covariance, iterate):
    row = lax.axis_index("row")
    depth = lax.axis_index("depth")
    x = (row // 2 % 2) * 2 + depth
    scal = jnp.stack([row % 2, depth, x, row // 4]).astype(jnp.int32)

    own_w = lax.dynamic_slice(iterate, (0, x * BLOCK), (ROWS, BLOCK))
    par_w = to_mirror(lax.dynamic_slice(iterate, (0, (3 - x) * BLOCK), (ROWS, BLOCK)))
    covariance, par_w = together((covariance, par_w))
    par_cov = to_mirror(covariance)
    par_iter = to_mirror(together((iterate, par_cov))[0])
    own_a = transposed(scal, covariance)
    par_a = transposed(scal, par_cov)

    own_blocks = gathered(own_w, 4, 3)
    par_blocks = gathered(par_w, 3, 4)
    own_blocks[4] = own_blocks[-4]
    near, far = (0, 1, -1, 2, -2), (4, 3, -3)

    def first(group, gate):
        blocks = [own_blocks[k] for k in group], [par_blocks[k] for k in group]
        if gate is not None:
            blocks, gate = together((blocks, gate))
        return first_product(*blocks, own_a, par_a), gate

    near_sums, _ = first(near, None)
    far_sums, near_sums = first(far, near_sums)
    near_mine, far_mine = reduced(*near_sums), reduced(*far_sums)
    far_half = spread(far_mine)
    near_mine, far_half[1] = together((near_mine, far_half[1]))
    near_half = spread(near_mine)
    own_terms, par_terms = {}, {}
    for group, half in ((far, far_half), (near, near_half)):
        pieces = half + [to_core(piece) for piece in half]
        outs = second_product(scal, pieces, iterate, par_iter)
        for k, own, par in zip(group, *outs):
            own_terms[k], par_terms[k] = own, par
    par_terms[-4] = par_terms[4]
    own = scattered(own_terms, 4, 3)
    par = scattered(par_terms, 3, 4)
    half = ROWS // 2
    par_away, par_home = together((par[:half], par[half:]))
    own_away, own_home = together((own[:half], own[half:]))
    pieces = [own_home, to_x1(own_away), to_mirror(par_away), to_x2(par_home)]
    return last(scal, iterate, pieces)


def solution(mesh):
    in_specs = (P("row", "col"), P("row", "col"))
    out_specs = P(("row", "depth"), "col")
    return jax.shard_map(local, mesh=mesh, in_specs=in_specs, out_specs=out_specs, check_vma=False)
```

```python
import functools
import jax
import jax.numpy as jnp
from jax import lax
from jax.experimental import pallas as pl
from jax.experimental.pallas import tpu as pltpu
from jax.sharding import PartitionSpec as P

F32 = jnp.float32
BF16 = jnp.bfloat16
VMEM_LIMIT = 24 * 1024 * 1024
ROWS = 448
COLS = 896
PIECE = 112
BLOCK = 128
TURNS = (2, 1, 3, 0)
together = lax.optimization_barrier


def split(value):
    hi = value.astype(BF16)
    lo = (value - hi.astype(F32)).astype(BF16)
    return hi, lo


def dot3(a_hi, a_lo, b_hi, b_lo):
    dot = functools.partial(jnp.dot, preferred_element_type=F32)
    return dot(a_hi, b_hi) + (dot(a_hi, b_lo) + dot(a_lo, b_hi))


def params():
    return pltpu.CompilerParams(vmem_limit_bytes=VMEM_LIMIT)


def piece_row(scal, core, turn):
    return pl.multiple_of(core * ROWS + (scal[3] + turn) % 4 * PIECE, PIECE)


def transpose_kernel(scal, tile, hi, lo, turned):
    turned[...] = tile[...].T
    for half, core in enumerate((1 - scal[0], scal[0])):
        for k, turn in enumerate(TURNS):
            start = half * ROWS + k * PIECE
            rows = turned[pl.ds(piece_row(scal, core, turn), PIECE)]
            hi[start : start + PIECE], lo[start : start + PIECE] = split(rows)


def transposed(scal, tile):
    return pl.pallas_call(
        transpose_kernel,
        grid_spec=pltpu.PrefetchScalarGridSpec(
            num_scalar_prefetch=1,
            grid=(1,),
            in_specs=[pl.BlockSpec((ROWS, COLS), lambda i, s: (0, 0))],
            out_specs=[pl.BlockSpec((COLS, ROWS), lambda i, s: (0, 0))] * 2,
            scratch_shapes=[pltpu.VMEM((COLS, ROWS), F32)],
        ),
        out_shape=[jax.ShapeDtypeStruct((COLS, ROWS), BF16)] * 2,
        compiler_params=params(),
        cost_estimate=pl.CostEstimate(flops=0, bytes_accessed=1024, transcendentals=0),
        name="transpose_split",
    )(scal, tile)


def first_kernel(count, *refs):
    blocks, (own_hi, own_lo, par_hi, par_lo, send, keep, w_hi, w_lo) = refs[: 2 * count], refs[2 * count :]
    for k in range(count):
        cols = slice(k * BLOCK, k * BLOCK + BLOCK)
        w_hi[:ROWS, cols], w_lo[:ROWS, cols] = split(blocks[k][...])
        w_hi[ROWS:, cols], w_lo[ROWS:, cols] = split(blocks[count + k][...])
    for half, out in enumerate((send, keep)):
        rows = slice(half * ROWS, half * ROWS + ROWS)
        total = dot3(own_hi[rows], own_lo[rows], w_hi[:ROWS], w_lo[:ROWS])
        total += dot3(par_hi[rows], par_lo[rows], w_hi[ROWS:], w_lo[ROWS:])
        out[...] = total.reshape(out.shape)


def cost(width):
    return pl.CostEstimate(
        flops=width, bytes_accessed=width, transcendentals=0
    )


def first_product(own_blocks, par_blocks, own, par):
    count = len(own_blocks)
    width = count * BLOCK
    tile = pl.BlockSpec((COLS, ROWS), lambda m: (0, 0))
    whole = pl.BlockSpec((ROWS, BLOCK), lambda m: (0, 0))
    return pl.pallas_call(
        functools.partial(first_kernel, count),
        grid=(1,),
        in_specs=[whole] * (2 * count) + [tile] * 4,
        out_specs=[pl.BlockSpec((4, PIECE, width), lambda m: (0, 0, 0))] * 2,
        scratch_shapes=[pltpu.VMEM((COLS, width), BF16)] * 2,
        out_shape=[jax.ShapeDtypeStruct((4, PIECE, width), F32)] * 2,
        compiler_params=params(),
        cost_estimate=cost(width),
        name="first_product",
    )(*own_blocks, *par_blocks, *own, *par)


def second_kernel(count, scal, *refs):
    pieces, tiles, refs = refs[:8], refs[8:10], refs[10:]
    outs, (p_hi, p_lo) = (refs[:count], refs[count : 2 * count]), refs[2 * count :]
    for half, core in enumerate((scal[0], 1 - scal[0])):
        for k, turn in enumerate((0, 2, 3, 1)):
            rows = pl.ds(piece_row(scal, core, turn), PIECE)
            p_hi[rows], p_lo[rows] = split(pieces[4 * half + k][...])
    for tile, out in zip(tiles, outs):
        for half, depth in enumerate((1 - scal[1], scal[1])):
            rows = pl.ds(pl.multiple_of(depth * (ROWS // 2), 8), ROWS // 2)
            total = dot3(*split(tile[rows]), p_hi[...], p_lo[...])
            rows = slice(half * (ROWS // 2), (half + 1) * (ROWS // 2))
            for k in range(count):
                out[k][rows] = total[:, k * BLOCK : k * BLOCK + BLOCK]


def second_product(scal, pieces, own, par):
    width = pieces[0].shape[1]
    count = width // BLOCK
    piece = pl.BlockSpec((PIECE, width), lambda m, s: (0, 0))
    tile = pl.BlockSpec((ROWS, COLS), lambda m, s: (0, 0))
    out = pl.pallas_call(
        functools.partial(second_kernel, count),
        grid_spec=pltpu.PrefetchScalarGridSpec(
            num_scalar_prefetch=1,
            grid=(1,),
            in_specs=[piece] * 8 + [tile, tile],
            out_specs=[pl.BlockSpec((ROWS, BLOCK), lambda m, s: (0, 0))] * (2 * count),
            scratch_shapes=[pltpu.VMEM((COLS, width), BF16)] * 2,
        ),
        out_shape=[jax.ShapeDtypeStruct((ROWS, BLOCK), F32)] * (2 * count),
        compiler_params=params(),
        cost_estimate=cost(width),
        name="second_product",
    )(scal, *pieces, own, par)
    return out[:count], out[count:]


def last_kernel(scal, iterate, *refs):
    pieces, out = refs[:4], refs[4]
    x = scal[2]
    rows = pl.ds(pl.multiple_of(scal[1] * 224, 8), 224)
    for piece, quarter in zip(pieces, (x, x ^ 1, 3 - x, x ^ 2)):
        cols = pl.ds(pl.multiple_of(quarter * BLOCK, BLOCK), BLOCK)
        out[:, cols] = 2.0 * iterate[rows, cols] - piece[...]


def last(scal, iterate, pieces):
    piece = pl.BlockSpec((224, BLOCK), lambda i, s: (0, 0))
    return pl.pallas_call(
        last_kernel,
        grid_spec=pltpu.PrefetchScalarGridSpec(
            num_scalar_prefetch=1,
            grid=(1,),
            in_specs=[pl.BlockSpec((ROWS, 512), lambda i, s: (0, 0))] + [piece] * 4,
            out_specs=pl.BlockSpec((224, 512), lambda i, s: (0, 0)),
        ),
        out_shape=jax.ShapeDtypeStruct((224, 512), F32),
        compiler_params=params(),
        cost_estimate=pl.CostEstimate(flops=0, bytes_accessed=1024, transcendentals=0),
        name="last",
    )(scal, iterate, *pieces)


def flip(mask):
    return [(r, r ^ mask) for r in range(16)]


def x_mirror():
    pairs = []
    for r in range(16):
        for d in range(2):
            x = 3 - ((r // 2 % 2) * 2 + d)
            pairs.append((r * 2 + d, ((r & 13) | (x // 2) * 2) * 2 + x % 2))
    return pairs


to_core = functools.partial(lax.ppermute, axis_name="row", perm=flip(1))
to_x2 = functools.partial(lax.ppermute, axis_name="row", perm=flip(2))
to_x1 = functools.partial(lax.ppermute, axis_name="depth", perm=[(0, 1), (1, 0)])
to_mirror = functools.partial(lax.ppermute, axis_name=("row", "depth"), perm=x_mirror())


def to_y(value, turn):
    return lax.ppermute(value, "row", [(r, (r + 4 * turn) % 16) for r in range(16)])


def to_z(value, turn):
    return lax.ppermute(value, "col", [(z, (z + turn) % 8) for z in range(8)])


def reduced(send, keep):
    got = to_core(send)
    pieces = together(tuple(keep[k] + got[k] for k in range(4)))
    got = together(tuple(to_y(pieces[k], TURNS[k]) for k in range(3)))
    return pieces[3] + got[0] + got[1] + got[2]


def spread(mine):
    return [mine] + [to_y(mine, turn) for turn in (2, 1, 3)]


def gathered(block, right, left):
    blocks = {0: block}
    for turn, steps in ((1, right), (-1, left)):
        value = block
        for step in range(1, steps + 1):
            value = to_z(value, turn)
            blocks[-turn * step] = value
    return blocks


def scattered(terms, right, left):
    total = terms[0]
    for turn, steps in ((1, right), (-1, left)):
        value = to_z(terms[turn * steps], turn)
        for step in range(steps - 1, 0, -1):
            value = to_z(value + terms[turn * step], turn)
        total = total + value
    return total


def local(covariance, iterate):
    row = lax.axis_index("row")
    depth = lax.axis_index("depth")
    x = (row // 2 % 2) * 2 + depth
    scal = jnp.stack([row % 2, depth, x, row // 4]).astype(jnp.int32)

    own_w = lax.dynamic_slice(iterate, (0, x * BLOCK), (ROWS, BLOCK))
    par_w = to_mirror(lax.dynamic_slice(iterate, (0, (3 - x) * BLOCK), (ROWS, BLOCK)))
    own_a = transposed(scal, covariance)
    covariance, par_w, own_a = together((covariance, par_w, own_a))
    par_cov = to_mirror(covariance)
    par_iter = to_mirror(together((iterate, par_cov))[0])
    par_a = transposed(scal, par_cov)

    own_blocks = gathered(own_w, 4, 3)
    par_blocks = gathered(par_w, 3, 4)
    own_blocks[4] = own_blocks[-4]
    near, far = (0, 1, -1, 2, -2), (4, 3, -3)

    def first(group, gate):
        blocks = [own_blocks[k] for k in group], [par_blocks[k] for k in group]
        if gate is not None:
            blocks, gate = together((blocks, gate))
        return first_product(*blocks, own_a, par_a), gate

    near_sums, _ = first(near, None)
    far_sums, near_sums = first(far, near_sums)
    near_mine, far_mine = reduced(*near_sums), reduced(*far_sums)
    near_mine, far_mine = together((near_mine, far_mine))
    far_half = spread(far_mine)
    near_mine, far_half = together((near_mine, far_half))
    near_half = spread(near_mine)
    own_terms, par_terms = {}, {}
    for group, half in ((far, far_half), (near, near_half)):
        pieces = half + [to_core(piece) for piece in half]
        outs = second_product(scal, pieces, iterate, par_iter)
        for k, own, par in zip(group, *outs):
            own_terms[k], par_terms[k] = own, par
    par_terms[-4] = par_terms[4]
    own = scattered(own_terms, 4, 3)
    par = scattered(par_terms, 3, 4)
    half = ROWS // 2
    par_away, par_home = together((par[:half], par[half:]))
    own_away, own_home = together((own[:half], own[half:]))
    pieces = [own_home, to_x1(own_away), to_mirror(par_away), to_x2(par_home)]
    return last(scal, iterate, pieces)


def solution(mesh):
    in_specs = (P("row", "col"), P("row", "col"))
    out_specs = P(("row", "depth"), "col")
    return jax.shard_map(local, mesh=mesh, in_specs=in_specs, out_specs=out_specs, check_vma=False)
```

```python
import functools
import jax
import jax.numpy as jnp
from jax import lax
from jax.experimental import pallas as pl
from jax.experimental.pallas import tpu as pltpu
from jax.sharding import PartitionSpec as P

F32 = jnp.float32
BF16 = jnp.bfloat16
VMEM_LIMIT = 24 * 1024 * 1024
ROWS = 448
COLS = 896
PIECE = 112
BLOCK = 128
TURNS = (2, 1, 3, 0)
together = lax.optimization_barrier


def split(value):
    hi = value.astype(BF16)
    lo = (value - hi.astype(F32)).astype(BF16)
    return hi, lo


def dot3(a_hi, a_lo, b_hi, b_lo):
    dot = functools.partial(jnp.dot, preferred_element_type=F32)
    return dot(a_hi, b_hi) + (dot(a_hi, b_lo) + dot(a_lo, b_hi))


def params():
    return pltpu.CompilerParams(vmem_limit_bytes=VMEM_LIMIT)


def piece_row(scal, core, turn):
    return pl.multiple_of(core * ROWS + (scal[3] + turn) % 4 * PIECE, PIECE)


def transpose_kernel(scal, tile, hi, lo, turned):
    turned[...] = tile[...].T
    for half, core in enumerate((1 - scal[0], scal[0])):
        for k, turn in enumerate(TURNS):
            start = half * ROWS + k * PIECE
            rows = turned[pl.ds(piece_row(scal, core, turn), PIECE)]
            hi[start : start + PIECE], lo[start : start + PIECE] = split(rows)


def transposed(scal, tile):
    return pl.pallas_call(
        transpose_kernel,
        grid_spec=pltpu.PrefetchScalarGridSpec(
            num_scalar_prefetch=1,
            grid=(1,),
            in_specs=[pl.BlockSpec((ROWS, COLS), lambda i, s: (0, 0))],
            out_specs=[pl.BlockSpec((COLS, ROWS), lambda i, s: (0, 0))] * 2,
            scratch_shapes=[pltpu.VMEM((COLS, ROWS), F32)],
        ),
        out_shape=[jax.ShapeDtypeStruct((COLS, ROWS), BF16)] * 2,
        compiler_params=params(),
        cost_estimate=pl.CostEstimate(flops=0, bytes_accessed=1024, transcendentals=0),
        name="transpose_split",
    )(scal, tile)


def first_kernel(count, *refs):
    blocks, (own_hi, own_lo, par_hi, par_lo, send, keep, w_hi, w_lo) = refs[: 2 * count], refs[2 * count :]
    for k in range(count):
        cols = slice(k * BLOCK, k * BLOCK + BLOCK)
        w_hi[:ROWS, cols], w_lo[:ROWS, cols] = split(blocks[k][...])
        w_hi[ROWS:, cols], w_lo[ROWS:, cols] = split(blocks[count + k][...])
    for half, out in enumerate((send, keep)):
        rows = slice(half * ROWS, half * ROWS + ROWS)
        total = dot3(own_hi[rows], own_lo[rows], w_hi[:ROWS], w_lo[:ROWS])
        total += dot3(par_hi[rows], par_lo[rows], w_hi[ROWS:], w_lo[ROWS:])
        out[...] = total.reshape(out.shape)


def cost(width):
    return pl.CostEstimate(
        flops=width, bytes_accessed=width, transcendentals=0
    )


def first_product(own_blocks, par_blocks, own, par):
    count = len(own_blocks)
    width = count * BLOCK
    tile = pl.BlockSpec((COLS, ROWS), lambda m: (0, 0))
    whole = pl.BlockSpec((ROWS, BLOCK), lambda m: (0, 0))
    return pl.pallas_call(
        functools.partial(first_kernel, count),
        grid=(1,),
        in_specs=[whole] * (2 * count) + [tile] * 4,
        out_specs=[pl.BlockSpec((4, PIECE, width), lambda m: (0, 0, 0))] * 2,
        scratch_shapes=[pltpu.VMEM((COLS, width), BF16)] * 2,
        out_shape=[jax.ShapeDtypeStruct((4, PIECE, width), F32)] * 2,
        compiler_params=params(),
        cost_estimate=cost(width),
        name="first_product",
    )(*own_blocks, *par_blocks, *own, *par)


def second_kernel(count, scal, *refs):
    pieces, tiles, refs = refs[:8], refs[8:10], refs[10:]
    outs, (p_hi, p_lo) = (refs[:count], refs[count : 2 * count]), refs[2 * count :]
    for half, core in enumerate((scal[0], 1 - scal[0])):
        for k, turn in enumerate((0, 2, 3, 1)):
            rows = pl.ds(piece_row(scal, core, turn), PIECE)
            p_hi[rows], p_lo[rows] = split(pieces[4 * half + k][...])
    for tile, out in zip(tiles, outs):
        for half, depth in enumerate((1 - scal[1], scal[1])):
            rows = pl.ds(pl.multiple_of(depth * (ROWS // 2), 8), ROWS // 2)
            total = dot3(*split(tile[rows]), p_hi[...], p_lo[...])
            rows = slice(half * (ROWS // 2), (half + 1) * (ROWS // 2))
            for k in range(count):
                out[k][rows] = total[:, k * BLOCK : k * BLOCK + BLOCK]


def second_product(scal, pieces, own, par):
    width = pieces[0].shape[1]
    count = width // BLOCK
    piece = pl.BlockSpec((PIECE, width), lambda m, s: (0, 0))
    tile = pl.BlockSpec((ROWS, COLS), lambda m, s: (0, 0))
    out = pl.pallas_call(
        functools.partial(second_kernel, count),
        grid_spec=pltpu.PrefetchScalarGridSpec(
            num_scalar_prefetch=1,
            grid=(1,),
            in_specs=[piece] * 8 + [tile, tile],
            out_specs=[pl.BlockSpec((ROWS, BLOCK), lambda m, s: (0, 0))] * (2 * count),
            scratch_shapes=[pltpu.VMEM((COLS, width), BF16)] * 2,
        ),
        out_shape=[jax.ShapeDtypeStruct((ROWS, BLOCK), F32)] * (2 * count),
        compiler_params=params(),
        cost_estimate=cost(width),
        name="second_product",
    )(scal, *pieces, own, par)
    return out[:count], out[count:]


def last_kernel(scal, iterate, *refs):
    pieces, out = refs[:4], refs[4]
    x = scal[2]
    rows = pl.ds(pl.multiple_of(scal[1] * 224, 8), 224)
    for piece, quarter in zip(pieces, (x, x ^ 1, 3 - x, x ^ 2)):
        cols = pl.ds(pl.multiple_of(quarter * BLOCK, BLOCK), BLOCK)
        out[:, cols] = 2.0 * iterate[rows, cols] - piece[...]


def last(scal, iterate, pieces):
    piece = pl.BlockSpec((224, BLOCK), lambda i, s: (0, 0))
    return pl.pallas_call(
        last_kernel,
        grid_spec=pltpu.PrefetchScalarGridSpec(
            num_scalar_prefetch=1,
            grid=(1,),
            in_specs=[pl.BlockSpec((ROWS, 512), lambda i, s: (0, 0))] + [piece] * 4,
            out_specs=pl.BlockSpec((224, 512), lambda i, s: (0, 0)),
        ),
        out_shape=jax.ShapeDtypeStruct((224, 512), F32),
        compiler_params=params(),
        cost_estimate=pl.CostEstimate(flops=0, bytes_accessed=1024, transcendentals=0),
        name="last",
    )(scal, iterate, *pieces)


def flip(mask):
    return [(r, r ^ mask) for r in range(16)]


def x_mirror():
    pairs = []
    for r in range(16):
        for d in range(2):
            x = 3 - ((r // 2 % 2) * 2 + d)
            pairs.append((r * 2 + d, ((r & 13) | (x // 2) * 2) * 2 + x % 2))
    return pairs


to_core = functools.partial(lax.ppermute, axis_name="row", perm=flip(1))
to_x2 = functools.partial(lax.ppermute, axis_name="row", perm=flip(2))
to_x1 = functools.partial(lax.ppermute, axis_name="depth", perm=[(0, 1), (1, 0)])
to_mirror = functools.partial(lax.ppermute, axis_name=("row", "depth"), perm=x_mirror())


def to_y(value, turn):
    return lax.ppermute(value, "row", [(r, (r + 4 * turn) % 16) for r in range(16)])


def to_z(value, turn):
    return lax.ppermute(value, "col", [(z, (z + turn) % 8) for z in range(8)])


def reduced(send, keep):
    got = to_core(send)
    pieces = together(tuple(keep[k] + got[k] for k in range(4)))
    got = together(tuple(to_y(pieces[k], TURNS[k]) for k in range(3)))
    return pieces[3] + got[0] + got[1] + got[2]


def spread(mine):
    return [mine] + [to_y(mine, turn) for turn in (2, 1, 3)]


def gathered(block, right, left):
    blocks = {0: block}
    for turn, steps in ((1, right), (-1, left)):
        value = block
        for step in range(1, steps + 1):
            value = to_z(value, turn)
            blocks[-turn * step] = value
    return blocks


def scattered(terms, right, left):
    total = terms[0]
    for turn, steps in ((1, right), (-1, left)):
        value = to_z(terms[turn * steps], turn)
        for step in range(steps - 1, 0, -1):
            value = to_z(value + terms[turn * step], turn)
        total = total + value
    return total


def local(covariance, iterate):
    row = lax.axis_index("row")
    depth = lax.axis_index("depth")
    x = (row // 2 % 2) * 2 + depth
    scal = jnp.stack([row % 2, depth, x, row // 4]).astype(jnp.int32)

    own_w = lax.dynamic_slice(iterate, (0, x * BLOCK), (ROWS, BLOCK))
    par_w = to_mirror(lax.dynamic_slice(iterate, (0, (3 - x) * BLOCK), (ROWS, BLOCK)))
    own_a = transposed(scal, covariance)
    covariance, par_w, own_a = together((covariance, par_w, own_a))
    par_cov = to_mirror(covariance)
    par_iter = to_mirror(together((iterate, par_cov))[0])
    par_a = transposed(scal, par_cov)

    own_blocks = gathered(own_w, 4, 3)
    par_blocks = gathered(par_w, 3, 4)
    own_blocks[4] = own_blocks[-4]
    near, far = (0, 1, -1, 2, -2), (4, 3, -3)

    def first(group, gate):
        blocks = [own_blocks[k] for k in group], [par_blocks[k] for k in group]
        if gate is not None:
            blocks, gate = together((blocks, gate))
        return first_product(*blocks, own_a, par_a), gate

    near_sums, _ = first(near, None)
    far_sums, near_sums = first(far, near_sums)
    near_mine, far_mine = reduced(*near_sums), reduced(*far_sums)
    far_half = spread(far_mine)
    near_mine, far_half = together((near_mine, far_half))
    near_half = spread(near_mine)
    own_terms, par_terms = {}, {}
    for group, half in ((far, far_half), (near, near_half)):
        pieces = half + [to_core(piece) for piece in half]
        outs = second_product(scal, pieces, iterate, par_iter)
        for k, own, par in zip(group, *outs):
            own_terms[k], par_terms[k] = own, par
    par_terms[-4] = par_terms[4]
    own = scattered(own_terms, 4, 3)
    par = scattered(par_terms, 3, 4)
    half = ROWS // 2
    par_away, par_home = together((par[:half], par[half:]))
    own_away, own_home = together((own[:half], own[half:]))
    pieces = [own_home, to_x1(own_away), to_mirror(par_away), to_x2(par_home)]
    return last(scal, iterate, pieces)


def solution(mesh):
    in_specs = (P("row", "col"), P("row", "col"))
    out_specs = P(("row", "depth"), "col")
    return jax.shard_map(local, mesh=mesh, in_specs=in_specs, out_specs=out_specs, check_vma=False)
```

```python
import functools
import jax
import jax.numpy as jnp
from jax import lax
from jax.experimental import pallas as pl
from jax.experimental.pallas import tpu as pltpu
from jax.sharding import PartitionSpec as P

F32 = jnp.float32
BF16 = jnp.bfloat16
VMEM_LIMIT = 24 * 1024 * 1024
ROWS = 448
COLS = 896
PIECE = 112
BLOCK = 128
TURNS = (2, 1, 3, 0)
together = lax.optimization_barrier


def split(value):
    hi = value.astype(BF16)
    lo = (value - hi.astype(F32)).astype(BF16)
    return hi, lo


def dot3(a_hi, a_lo, b_hi, b_lo):
    dot = functools.partial(jnp.dot, preferred_element_type=F32)
    return dot(a_hi, b_hi) + (dot(a_hi, b_lo) + dot(a_lo, b_hi))


def params():
    return pltpu.CompilerParams(vmem_limit_bytes=VMEM_LIMIT)


def piece_row(scal, core, turn):
    return pl.multiple_of(core * ROWS + (scal[3] + turn) % 4 * PIECE, PIECE)


def transpose_kernel(scal, tile, hi, lo, turned):
    turned[...] = tile[...].T
    for half, core in enumerate((1 - scal[0], scal[0])):
        for k, turn in enumerate(TURNS):
            start = half * ROWS + k * PIECE
            rows = turned[pl.ds(piece_row(scal, core, turn), PIECE)]
            hi[start : start + PIECE], lo[start : start + PIECE] = split(rows)


def transposed(scal, tile):
    return pl.pallas_call(
        transpose_kernel,
        grid_spec=pltpu.PrefetchScalarGridSpec(
            num_scalar_prefetch=1,
            grid=(1,),
            in_specs=[pl.BlockSpec((ROWS, COLS), lambda i, s: (0, 0))],
            out_specs=[pl.BlockSpec((COLS, ROWS), lambda i, s: (0, 0))] * 2,
            scratch_shapes=[pltpu.VMEM((COLS, ROWS), F32)],
        ),
        out_shape=[jax.ShapeDtypeStruct((COLS, ROWS), BF16)] * 2,
        compiler_params=params(),
        cost_estimate=pl.CostEstimate(flops=0, bytes_accessed=1024, transcendentals=0),
        name="transpose_split",
    )(scal, tile)


def first_kernel(count, *refs):
    blocks, (own_hi, own_lo, par_hi, par_lo, send, keep, w_hi, w_lo) = refs[: 2 * count], refs[2 * count :]
    for k in range(count):
        cols = slice(k * BLOCK, k * BLOCK + BLOCK)
        w_hi[:ROWS, cols], w_lo[:ROWS, cols] = split(blocks[k][...])
        w_hi[ROWS:, cols], w_lo[ROWS:, cols] = split(blocks[count + k][...])
    for half, out in enumerate((send, keep)):
        rows = slice(half * ROWS, half * ROWS + ROWS)
        total = dot3(own_hi[rows], own_lo[rows], w_hi[:ROWS], w_lo[:ROWS])
        total += dot3(par_hi[rows], par_lo[rows], w_hi[ROWS:], w_lo[ROWS:])
        out[...] = total.reshape(out.shape)


def cost(width):
    return pl.CostEstimate(
        flops=width, bytes_accessed=width, transcendentals=0
    )


def first_product(own_blocks, par_blocks, own, par):
    count = len(own_blocks)
    width = count * BLOCK
    tile = pl.BlockSpec((COLS, ROWS), lambda m: (0, 0))
    whole = pl.BlockSpec((ROWS, BLOCK), lambda m: (0, 0))
    return pl.pallas_call(
        functools.partial(first_kernel, count),
        grid=(1,),
        in_specs=[whole] * (2 * count) + [tile] * 4,
        out_specs=[pl.BlockSpec((4, PIECE, width), lambda m: (0, 0, 0))] * 2,
        scratch_shapes=[pltpu.VMEM((COLS, width), BF16)] * 2,
        out_shape=[jax.ShapeDtypeStruct((4, PIECE, width), F32)] * 2,
        compiler_params=params(),
        cost_estimate=cost(width),
        name="first_product",
    )(*own_blocks, *par_blocks, *own, *par)


def second_kernel(first, count, scal, *refs):
    taken = slice(first * BLOCK, (first + count) * BLOCK)
    pieces, tiles, refs = refs[:8], refs[8:10], refs[10:]
    outs, (p_hi, p_lo) = (refs[:count], refs[count : 2 * count]), refs[2 * count :]
    for half, core in enumerate((scal[0], 1 - scal[0])):
        for k, turn in enumerate((0, 2, 3, 1)):
            rows = pl.ds(piece_row(scal, core, turn), PIECE)
            p_hi[rows], p_lo[rows] = split(pieces[4 * half + k][:, taken])
    for tile, out in zip(tiles, outs):
        for half, depth in enumerate((1 - scal[1], scal[1])):
            rows = pl.ds(pl.multiple_of(depth * (ROWS // 2), 8), ROWS // 2)
            total = dot3(*split(tile[rows]), p_hi[...], p_lo[...])
            rows = slice(half * (ROWS // 2), (half + 1) * (ROWS // 2))
            for k in range(count):
                out[k][rows] = total[:, k * BLOCK : k * BLOCK + BLOCK]


def second_product(scal, pieces, own, par, first, count):
    width = count * BLOCK
    piece = pl.BlockSpec(pieces[0].shape, lambda m, s: (0, 0))
    tile = pl.BlockSpec((ROWS, COLS), lambda m, s: (0, 0))
    out = pl.pallas_call(
        functools.partial(second_kernel, first, count),
        grid_spec=pltpu.PrefetchScalarGridSpec(
            num_scalar_prefetch=1,
            grid=(1,),
            in_specs=[piece] * 8 + [tile, tile],
            out_specs=[pl.BlockSpec((ROWS, BLOCK), lambda m, s: (0, 0))] * (2 * count),
            scratch_shapes=[pltpu.VMEM((COLS, width), BF16)] * 2,
        ),
        out_shape=[jax.ShapeDtypeStruct((ROWS, BLOCK), F32)] * (2 * count),
        compiler_params=params(),
        cost_estimate=cost(width),
        name="second_product",
    )(scal, *pieces, own, par)
    return out[:count], out[count:]


def last_kernel(scal, iterate, *refs):
    pieces, out = refs[:4], refs[4]
    x = scal[2]
    rows = pl.ds(pl.multiple_of(scal[1] * 224, 8), 224)
    for piece, quarter in zip(pieces, (x, x ^ 1, 3 - x, x ^ 2)):
        cols = pl.ds(pl.multiple_of(quarter * BLOCK, BLOCK), BLOCK)
        out[:, cols] = 2.0 * iterate[rows, cols] - piece[...]


def last(scal, iterate, pieces):
    piece = pl.BlockSpec((224, BLOCK), lambda i, s: (0, 0))
    return pl.pallas_call(
        last_kernel,
        grid_spec=pltpu.PrefetchScalarGridSpec(
            num_scalar_prefetch=1,
            grid=(1,),
            in_specs=[pl.BlockSpec((ROWS, 512), lambda i, s: (0, 0))] + [piece] * 4,
            out_specs=pl.BlockSpec((224, 512), lambda i, s: (0, 0)),
        ),
        out_shape=jax.ShapeDtypeStruct((224, 512), F32),
        compiler_params=params(),
        cost_estimate=pl.CostEstimate(flops=0, bytes_accessed=1024, transcendentals=0),
        name="last",
    )(scal, iterate, *pieces)


def flip(mask):
    return [(r, r ^ mask) for r in range(16)]


def x_mirror():
    pairs = []
    for r in range(16):
        for d in range(2):
            x = 3 - ((r // 2 % 2) * 2 + d)
            pairs.append((r * 2 + d, ((r & 13) | (x // 2) * 2) * 2 + x % 2))
    return pairs


to_core = functools.partial(lax.ppermute, axis_name="row", perm=flip(1))
to_x2 = functools.partial(lax.ppermute, axis_name="row", perm=flip(2))
to_x1 = functools.partial(lax.ppermute, axis_name="depth", perm=[(0, 1), (1, 0)])
to_mirror = functools.partial(lax.ppermute, axis_name=("row", "depth"), perm=x_mirror())


def to_y(value, turn):
    return lax.ppermute(value, "row", [(r, (r + 4 * turn) % 16) for r in range(16)])


def to_z(value, turn):
    return lax.ppermute(value, "col", [(z, (z + turn) % 8) for z in range(8)])


def reduced(send, keep):
    got = to_core(send)
    pieces = together(tuple(keep[k] + got[k] for k in range(4)))
    got = together(tuple(to_y(pieces[k], TURNS[k]) for k in range(3)))
    return pieces[3] + got[0] + got[1] + got[2]


def spread(mine):
    return [mine] + [to_y(mine, turn) for turn in (2, 1, 3)]


def gathered(block, right, left):
    blocks = {0: block}
    for turn, steps in ((1, right), (-1, left)):
        value = block
        for step in range(1, steps + 1):
            value = to_z(value, turn)
            blocks[-turn * step] = value
    return blocks


def scattered(terms, right, left):
    total = terms[0]
    for turn, steps in ((1, right), (-1, left)):
        value = to_z(terms[turn * steps], turn)
        for step in range(steps - 1, 0, -1):
            value = to_z(value + terms[turn * step], turn)
        total = total + value
    return total


def local(covariance, iterate):
    row = lax.axis_index("row")
    depth = lax.axis_index("depth")
    x = (row // 2 % 2) * 2 + depth
    scal = jnp.stack([row % 2, depth, x, row // 4]).astype(jnp.int32)

    own_w = lax.dynamic_slice(iterate, (0, x * BLOCK), (ROWS, BLOCK))
    par_w = to_mirror(lax.dynamic_slice(iterate, (0, (3 - x) * BLOCK), (ROWS, BLOCK)))
    own_a = transposed(scal, covariance)
    covariance, par_w, own_a = together((covariance, par_w, own_a))
    par_cov = to_mirror(covariance)
    par_iter = to_mirror(together((iterate, par_cov))[0])
    par_a = transposed(scal, par_cov)

    own_blocks = gathered(own_w, 4, 3)
    par_blocks = gathered(par_w, 3, 4)
    own_blocks[4] = own_blocks[-4]
    near, far = (2, -2, 0, 1, -1), (4, 3, -3)

    def first(group, gate):
        blocks = [own_blocks[k] for k in group], [par_blocks[k] for k in group]
        if gate is not None:
            blocks, gate = together((blocks, gate))
        return first_product(*blocks, own_a, par_a), gate

    near_sums, _ = first(near, None)
    far_sums, near_sums = first(far, near_sums)
    near_mine, far_mine = reduced(*near_sums), reduced(*far_sums)
    far_half = spread(far_mine)
    near_mine, far_half = together((near_mine, far_half))
    near_half = spread(near_mine)
    own_terms, par_terms = {}, {}
    for group, half in ((far, far_half), (near, near_half)):
        pieces = half + [to_core(piece) for piece in half]
        parts = ((0, 3),) if group == far else ((0, 2), (2, 3))
        for first_block, count in parts:
            outs = second_product(scal, pieces, iterate, par_iter, first_block, count)
            for k, own, par in zip(group[first_block : first_block + count], *outs):
                own_terms[k], par_terms[k] = own, par
    par_terms[-4] = par_terms[4]
    own = scattered(own_terms, 4, 3)
    par = scattered(par_terms, 3, 4)
    half = ROWS // 2
    par_away, par_home = together((par[:half], par[half:]))
    own_away, own_home = together((own[:half], own[half:]))
    pieces = [own_home, to_x1(own_away), to_mirror(par_away), to_x2(par_home)]
    return last(scal, iterate, pieces)


def solution(mesh):
    in_specs = (P("row", "col"), P("row", "col"))
    out_specs = P(("row", "depth"), "col")
    return jax.shard_map(local, mesh=mesh, in_specs=in_specs, out_specs=out_specs, check_vma=False)
```
